32 devices in a mesh: group: 2 (over y), chan: 4 (over z), frame: 2 (over x), sub: 2 (over core).
Axes of the slice: x: 2, y: 2, z: 4, core: 2. Of those that a mesh axis runs over, the one named last changes fastest.
Arguments:
- rf: bfloat16 [32768, 512], P(('group', 'chan', 'sub'), 'frame'), parts along dimension 0, may hold values from -10 to 10
- weights: bfloat16 [8, 2, 2, 128, 128], P(('chan', 'sub')), may hold values from -0.125 to 0.125
- sample_block: int32 [8, 2, 2], P(('chan', 'sub')), may hold values from 0 to 15
- live: int32 [8, 2, 2], P(('chan', 'sub')), may hold values 0 or 1
- rank: int32 [2], P('group'), parts along dimension 0, may hold values from 16 to 32
Outputs:
- power: float32 [16, 2, 16], P(('group', 'chan', 'sub'), 'frame'), parts along dimension 0
The draws below stay inside these ranges and needn't reach their ends.
There are 2 independent parts, one for each index of `group`. The reference program is written for one: setup_inputs(seed, part) draws one part's arguments, and reference() takes and returns one part's arrays. A program takes and returns all parts, laid end to end along the dimension named above; an argument that names none is the same for every part. Nothing has to cross between parts.
Inputs may be any that keep to these rules, and one draw needn't show every extreme that they name: `sample_block`: index of a delay window within the channel's trace. `rank`: number of leading basis columns removed as clutter.
All inputs are finite; a program needn't handle non-finite values. No bound on the sum of `live` on one device may be relied on, other than what follows from the above.
Results may differ from the reference program's by a relative error of at most 0.0003.
Values sent between devices are 32-bit elements; how exact they have to be, the bound alone decides.
A program may use at most 64 MiB of HBM per device.

```python
import math
import jax
import jax.numpy as jnp
from jax import lax

F = 512
SAMPLES = 2048
SB = 128
VB = 128
NPER = 2
RMAX = 32
VOX_DEV = 16
CB = 8
CHANNELS = 8
NSB = 16
V = 256
VBLK = 2
N_FRAME = 2


def draw_rf(key, part):
    key = jax.random.fold_in(key, 11)
    key_noise, key_amp, key_freq, key_phase = jax.random.split(key, 4)
    rows = CHANNELS * SAMPLES
    noise = jnp.clip(jax.random.normal(key_noise, (rows, F), jnp.float32), -6.0, 6.0)
    amplitude = jnp.exp(jax.random.uniform(key_amp, (rows, 1), jnp.float32, 0.0, math.log(4.0)))
    omega = jax.random.uniform(key_freq, (rows, 1), jnp.float32, 0.0, math.pi * RMAX / F)
    phase = jax.random.uniform(key_phase, (rows, 1), jnp.float32, -math.pi, math.pi)
    frames = jnp.arange(F, dtype=jnp.float32)[None, :] + 0.5
    return (noise + amplitude * jnp.cos(omega * frames + phase)).astype(jnp.bfloat16)


def touch_ends(array, rng, smallest, largest):
    index_at = [jax.random.randint(jax.random.fold_in(rng, axis), (), 0, length) for axis, length in enumerate(array.shape)]
    longest = array.shape.index(max(array.shape))
    neighbour = index_at[:longest] + [(index_at[longest] + 1) % array.shape[longest]] + index_at[longest + 1:]
    return array.at[tuple(index_at)].set(smallest).at[tuple(neighbour)].set(largest)


def levels(stream_key, extent, shards, least, high):
    factor_of, own = 1.0, jax.random.fold_in(stream_key, 6)
    for dim, parts in shards:
        steps = jnp.exp(jax.random.uniform(jax.random.fold_in(own, dim), (parts,), jnp.float32, least / len(shards), high / len(shards)))
        factor_of = factor_of * jnp.repeat(steps, extent[dim] // parts).reshape([-1 if axis == dim else 1 for axis in range(len(extent))])
    return factor_of


def centred(rng, dims, spread, limit, cuts=(), kind=jnp.bfloat16):
    values = spread * jax.random.normal(rng, dims, jnp.float32)
    if cuts:
        values = values * levels(rng, dims, cuts, -0.22, 0.18)
    return jnp.clip(values, -limit, limit).astype(kind)


def setup_inputs(seed: int = 0, part: int = 0) -> dict:
    streams_of = jax.random.split(jax.random.key(seed), 6)
    own_keys = jax.random.split(jax.random.fold_in(streams_of[5], part), 6)
    return {
        "rf": draw_rf(jax.random.fold_in(jax.random.fold_in(streams_of[5], part), 71), part),
        "weights": centred(streams_of[1], (CB, VBLK, NPER, SB, VB), (NPER * SB * CB) ** -0.5, 0.125, ((0, 8),)),
        "sample_block": touch_ends(jax.random.randint(streams_of[2], (CB, VBLK, NPER), 0, NSB), jax.random.fold_in(streams_of[2], 1), 0, NSB - 1).astype(jnp.int32),
        "live": touch_ends((jax.random.randint(streams_of[3], (CB, VBLK, NPER), 0, 4) < 3).astype(jnp.int32), jax.random.fold_in(streams_of[3], 1), 0, 1),
        "rank": jax.random.randint(own_keys[4], (1,), RMAX // 2, RMAX + 1).astype(jnp.int32),
    }


def start_basis():
    frames = jnp.arange(F, dtype=jnp.float32)[:, None] + 0.5
    orders = jnp.arange(RMAX, dtype=jnp.float32)[None, :]
    return jnp.cos(math.pi * frames * orders / F) * math.sqrt(2.0 / F)

def clutter_basis(subspace, rank):
    keep = (jnp.arange(RMAX) < rank[0]).astype(jnp.float32)
    masked = subspace * keep[None, :]
    matrix = jnp.dot(masked.T, masked, precision=lax.Precision.HIGHEST) + jnp.diag(1.0 - keep)
    lower = jnp.linalg.cholesky(matrix)
    return lax.linalg.triangular_solve(lower, masked, left_side=False, lower=True, transpose_a=True)

def reference(rf, weights, sample_block, live, rank):
    blocks = rf.reshape(CB, NSB, SB, F)

    def accumulate(total, items):
        block_set, weight_set, index_set, live_set = items
        gathered = jnp.take(block_set, index_set, axis=0).astype(jnp.float32)
        masked = (weight_set * live_set[:, :, None, None].astype(jnp.bfloat16)).astype(jnp.float32)
        return (total + jnp.einsum('bpsc,bpsf->bcf', masked, gathered, precision=lax.Precision.HIGHEST), None)
    total = jnp.zeros((VBLK, VB, F), jnp.float32)
    total, unused = lax.scan(accumulate, total, (blocks, weights, sample_block, live))
    signal = total.reshape(V, F)
    gram = jnp.dot(signal.T, signal, precision=lax.Precision.HIGHEST)
    subspace = jnp.dot(gram, start_basis(), precision=lax.Precision.HIGHEST)
    basis = clutter_basis(subspace, rank)
    coeffs = jnp.dot(signal, basis, precision=lax.Precision.HIGHEST)
    clean = signal - jnp.dot(coeffs, basis.T, precision=lax.Precision.HIGHEST)
    power = lax.optimization_barrier(jnp.mean(clean * clean, axis=1))
    return power.reshape(CB, N_FRAME, VOX_DEV)
```

```python
import functools
import math

import jax
import jax.numpy as jnp
import ml_dtypes
import numpy as np
from jax import lax
from jax.experimental import pallas as pl
from jax.experimental.pallas import tpu as pltpu
from jax.sharding import PartitionSpec as P

RMAX = 32
LANES = 128
SUBL = 8
F32 = jnp.float32
BF16 = jnp.bfloat16
NT = (((1,), (1,)), ((), ()))
NN = (((1,), (0,)), ((), ()))
TN = (((0,), (0,)), ((), ()))


def start_parts(frames):
    at = np.arange(frames, dtype=np.float64)[None, :] + 0.5
    order = np.arange(RMAX, dtype=np.float64)[:, None]
    start = np.cos(math.pi * at * order / frames) * math.sqrt(2.0 / frames)
    high = start.astype(ml_dtypes.bfloat16)
    low = (start - high.astype(np.float64)).astype(ml_dtypes.bfloat16)
    return np.concatenate([high, low], axis=0)


def split(x):
    high = x.astype(BF16)
    return high, (x - high.astype(F32)).astype(BF16)


def mm(a, b, dims):
    return lax.dot_general(a, b, dims, preferred_element_type=F32)


def each(count, body):
    if count <= 16:
        for i in range(count):
            body(i)
    else:
        lax.fori_loop(0, count, lambda i, c: (body(i), c)[1], 0)


def kernel(
    dims,
    index_ref,
    live_ref,
    rank_ref,
    rf_hbm,
    w_hbm,
    start_hbm,
    out_ref,
    rf,
    w,
    start,
    part,
    slots,
    mpart,
    mslots,
    full,
    load_sem,
    send_sem,
    recv_sem,
):
    n_chan, n_sub, n_frame = dims
    n = n_chan * n_sub * n_frame
    num_blocks, num_slots, depth, width = w.shape
    vox = slots.shape[1]
    n_lane = full.shape[0]
    n_row = RMAX // SUBL
    tiles = n_lane * n_row
    stride = n // tiles
    group = lax.axis_index("group")
    me = (lax.axis_index("chan") * n_sub + lax.axis_index("sub")) * n_frame + lax.axis_index("frame")

    def place(d):
        return (group, d // (n_sub * n_frame), lax.rem(d, n_frame), lax.rem(d // n_frame, n_sub))

    def send(src, dst, phase, d):
        return pltpu.make_async_remote_copy(
            src_ref=src,
            dst_ref=dst,
            send_sem=send_sem.at[phase],
            recv_sem=recv_sem.at[phase],
            device_id=place(d),
            device_id_type=pl.DeviceIdType.MESH,
        )

    loads = [
        pltpu.make_async_copy(src, dst, load_sem.at[i])
        for i, (src, dst) in enumerate(((rf_hbm, rf), (w_hbm, w), (start_hbm, start)))
    ]
    for load in loads:
        load.start()

    barrier = pltpu.get_barrier_semaphore()
    each(
        n - 1,
        lambda r: pl.semaphore_signal(
            barrier, inc=1, device_id=place(lax.rem(me + r + 1, n)), device_id_type=pl.DeviceIdType.MESH
        ),
    )
    for load in loads:
        load.wait()

    def beam(b):
        total = None
        for p in range(num_slots):
            term = mm(w[b, p], rf[index_ref[0, b, p]], TN) * live_ref[0, b, p].astype(F32)
            total = term if total is None else total + term
        part[pl.ds(b * width, width), :] = total

    each(num_blocks, beam)
    pl.semaphore_wait(barrier, n - 1)

    def rows_of(d):
        return part.at[pl.ds(pl.multiple_of(d * vox, vox), vox), :]

    def scatter(r):
        d = lax.rem(me + r + 1, n)
        send(rows_of(d), slots.at[me], 0, d).start()

    each(n - 1, scatter)
    slots[me] = rows_of(me)[...]
    send(slots.at[pl.ds(0, n - 1)], slots.at[pl.ds(0, n - 1)], 0, me).wait_recv()

    def gather_frame(q):
        if n <= 16:
            total = slots[q]
            for c in range(1, n // n_frame):
                total = total + slots[c * n_frame + q]
            return total
        return lax.fori_loop(1, n // n_frame, lambda c, t: t + slots[c * n_frame + q], slots[q])

    signal = jnp.concatenate([gather_frame(q) for q in range(n_frame)], axis=1)

    s_high, s_low = split(signal)
    t_high, t_low = start[:RMAX, :], start[RMAX:, :]
    rep_high = jnp.concatenate([s_high] * 4, axis=0)
    rep_low = jnp.concatenate([s_low] * 4, axis=0)
    proj = mm(t_high, rep_high, NT) + mm(t_low, rep_high, NT) + mm(t_high, rep_low, NT)
    p_high = proj.astype(BF16).astype(F32)
    lane = lax.broadcasted_iota(jnp.int32, proj.shape, 1)
    proj = jnp.where(lane < 2 * vox, p_high, proj - p_high).astype(BF16)
    sub_part = mm(proj, jnp.concatenate([s_high, s_low] * 2, axis=0), NN)
    for j in range(n_lane):
        mpart[j] = sub_part[:, j * LANES : (j + 1) * LANES]

    def tile(ref, t):
        return ref.at[t // n_row, pl.ds(pl.multiple_of(lax.rem(t, n_row) * SUBL, SUBL), SUBL), :]

    first = me // stride
    reducer = lax.rem(me, stride) == 0

    def to_reducer(r):
        t = lax.rem(first + r + 1, tiles)
        send(tile(mpart, t), mslots.at[me], 1, t * stride).start()

    each(tiles - 1, to_reducer)
    if stride > 1:
        pl.when(jnp.logical_not(reducer))(lambda: to_reducer(tiles - 1))

    def reduce_tile():
        mslots[me] = tile(mpart, first)[...]
        send(mslots.at[pl.ds(0, n - 1)], mslots.at[pl.ds(0, n - 1)], 1, me).wait_recv()
        if n <= 16:
            total = mslots[0]
            for d in range(1, n):
                total = total + mslots[d]
        else:
            total = lax.fori_loop(1, n, lambda d, t: t + mslots[d], mslots[0])
        tile(full, first)[...] = total

        def spread(r):
            send(tile(full, first), tile(full, first), 2, lax.rem(me + r + 1, n)).start()

        each(n - 1, spread)

    if stride > 1:
        pl.when(reducer)(reduce_tile)
        got = mslots.at[pl.ds(0, tiles)]
        pl.when(jnp.logical_not(reducer))(lambda: send(got, got, 2, me).wait_recv())
    else:
        reduce_tile()
    got = mslots.at[pl.ds(0, tiles - 1)]
    if stride > 1:
        pl.when(reducer)(lambda: send(got, got, 2, me).wait_recv())
    else:
        send(got, got, 2, me).wait_recv()

    kept = lax.broadcasted_iota(jnp.int32, (RMAX, 1), 0) < rank_ref[0]
    sub = jnp.concatenate([full[j] for j in range(n_lane)], axis=1)
    sub = jnp.where(kept, sub, 0.0)
    m_high, m_low = split(sub)
    left_high = jnp.concatenate([m_high, s_high], axis=0)
    left_low = jnp.concatenate([m_low, s_low], axis=0)
    rep_high = jnp.concatenate([m_high] * 4, axis=0)
    rep_low = jnp.concatenate([m_low] * 4, axis=0)
    system = mm(left_high, rep_high, NT) + mm(left_low, rep_high, NT) + mm(left_high, rep_low, NT)
    row = lax.broadcasted_iota(jnp.int32, system.shape, 0)
    order = lax.rem(lax.broadcasted_iota(jnp.int32, system.shape, 1), RMAX)
    system = system + jnp.where((row == order) & (row >= rank_ref[0]), 1.0, 0.0)
    order = order[:1]
    for k in range(RMAX):
        at = k % SUBL
        if k and at == 0:
            system = system[SUBL:, :]
        inverse = 1.0 / system[at : at + 1, k : k + 1]
        here = order == k
        factor = jnp.where(here, -inverse, system[at : at + 1, :] * inverse)
        system = jnp.where(here, 0.0, system) - system[:, k : k + 1] * factor
    coeffs = system[SUBL:, :]
    c_high = coeffs.astype(BF16).astype(F32)
    lane = lax.broadcasted_iota(jnp.int32, coeffs.shape, 1)
    coeffs = jnp.where(lane < 2 * RMAX, c_high, coeffs - c_high).astype(BF16)
    clean = signal - mm(coeffs, jnp.concatenate([m_high, m_low] * 2, axis=0), NN)
    power = jnp.sum(clean * clean, axis=1, keepdims=True) * (1.0 / clean.shape[1])
    diagonal = lax.broadcasted_iota(jnp.int32, (vox, vox), 0) == lax.broadcasted_iota(jnp.int32, (vox, vox), 1)
    out_ref[...] = jnp.sum(jnp.where(diagonal, power, 0.0), axis=0, keepdims=True)[None]

    sent = slots.at[pl.ds(0, n - 1)]
    send(sent, sent, 0, me).wait_send()
    sent = mslots.at[pl.ds(0, tiles - 1)]
    send(sent, sent, 1, me).wait_send()
    if stride > 1:
        pl.when(jnp.logical_not(reducer))(lambda: send(mslots.at[0], mslots.at[0], 1, me).wait_send())
    sent = mslots.at[pl.ds(0, n - 1)]
    if stride > 1:
        pl.when(reducer)(lambda: send(sent, sent, 2, me).wait_send())
    else:
        send(sent, sent, 2, me).wait_send()


def shards(dims, rf, weights, sample_block, live, rank):
    n = math.prod(dims)
    _, num_blocks, num_slots, depth, width = weights.shape
    vox = num_blocks * width // n
    frames = rf.shape[1] * dims[2]
    n_lane = frames // LANES
    blocks = rf.reshape(rf.shape[0] // depth, depth, rf.shape[1])
    smem = pl.BlockSpec(memory_space=pltpu.SMEM)
    hbm = pl.BlockSpec(memory_space=pl.ANY)
    return pl.pallas_call(
        functools.partial(kernel, dims),
        out_shape=jax.ShapeDtypeStruct((1, 1, vox), F32),
        in_specs=[smem, smem, smem, hbm, hbm, hbm],
        out_specs=pl.BlockSpec(memory_space=pltpu.VMEM),
        scratch_shapes=[
            pltpu.VMEM(blocks.shape, BF16),
            pltpu.VMEM(weights.shape[1:], BF16),
            pltpu.VMEM((2 * RMAX, frames), BF16),
            pltpu.VMEM((num_blocks * width, rf.shape[1]), F32),
            pltpu.VMEM((n, vox, rf.shape[1]), F32),
            pltpu.VMEM((n_lane, RMAX, LANES), F32),
            pltpu.VMEM((n, SUBL, LANES), F32),
            pltpu.VMEM((n_lane, RMAX, LANES), F32),
            pltpu.SemaphoreType.DMA((3,)),
            pltpu.SemaphoreType.DMA((3,)),
            pltpu.SemaphoreType.DMA((3,)),
        ],
        compiler_params=pltpu.CompilerParams(
            collective_id=0, has_side_effects=True, vmem_limit_bytes=32 * 1024 * 1024
        ),
        name="power_doppler",
    )(sample_block, live, rank, blocks, weights[0], jnp.asarray(start_parts(frames)))


def solution(mesh):
    dims = (mesh.shape["chan"], mesh.shape["sub"], mesh.shape["frame"])
    return jax.shard_map(
        functools.partial(shards, dims),
        mesh=mesh,
        in_specs=(
            P(("group", "chan", "sub"), "frame"),
            P(("chan", "sub"), None, None, None, None),
            P(("chan", "sub"), None, None),
            P(("chan", "sub"), None, None),
            P("group"),
        ),
        out_specs=P(("group", "chan", "sub"), "frame", None),
        check_vma=False,
    )
```

```python
import functools
import math

import jax
import jax.numpy as jnp
import numpy as np
from jax import lax
from jax.experimental import pallas as pl
from jax.experimental.pallas import tpu as pltpu
from jax.sharding import PartitionSpec as P

RMAX = 32
LANES = 128
SUBL = 8
UNIT = 16
F32 = jnp.float32
BF16 = jnp.bfloat16
NT = (((1,), (1,)), ((), ()))
NN = (((1,), (0,)), ((), ()))
TN = (((0,), (0,)), ((), ()))


def start_basis(frames):
    at = np.arange(frames, dtype=np.float64)[None, :] + 0.5
    order = np.arange(RMAX, dtype=np.float64)[:, None]
    return (np.cos(math.pi * at * order / frames) * math.sqrt(2.0 / frames)).astype(np.float32)


def split(x):
    high = x.astype(BF16)
    return high, (x - high.astype(F32)).astype(BF16)


def mm(a, b, dims):
    return lax.dot_general(a, b, dims, preferred_element_type=F32)


def each(count, body):
    if count <= 16:
        for i in range(count):
            body(i)
    else:
        lax.fori_loop(0, count, lambda i, c: (body(i), c)[1], 0)


def kernel(
    dims,
    index_hbm,
    live_hbm,
    rank_hbm,
    rf_hbm,
    w_hbm,
    start_hbm,
    out_ref,
    index_ref,
    live_ref,
    rank_ref,
    rf,
    w,
    start,
    part,
    slots,
    mpart,
    mslots,
    full,
    load_sem,
    send_sem,
    recv_sem,
):
    n_chan, n_sub, n_frame = dims
    n = n_chan * n_sub * n_frame
    num_blocks, num_slots, depth, width = w.shape
    vox = slots.shape[1]
    n_lane = full.shape[0]
    group = lax.axis_index("group")
    me = (lax.axis_index("chan") * n_sub + lax.axis_index("sub")) * n_frame + lax.axis_index("frame")

    def partner(r):
        if not isinstance(r, int):
            return lax.rem(me + r, n)
        d, bit = me, 1
        while bit <= r:
            if r & bit:
                d = d + bit - 2 * bit * lax.rem(me // bit, 2)
            bit *= 2
        return d

    def place(d):
        return (group, d // (n_sub * n_frame), lax.rem(d, n_frame), lax.rem(d // n_frame, n_sub))

    def send(src, dst, phase, d):
        return pltpu.make_async_remote_copy(
            src_ref=src,
            dst_ref=dst,
            send_sem=send_sem.at[phase],
            recv_sem=recv_sem.at[phase],
            device_id=place(d),
            device_id_type=pl.DeviceIdType.MESH,
        )

    loads = [
        pltpu.make_async_copy(src, dst, load_sem.at[i])
        for i, (src, dst) in enumerate(
            (
                (index_hbm, index_ref),
                (live_hbm, live_ref),
                (rank_hbm, rank_ref),
                (rf_hbm, rf),
                (w_hbm, w),
                (start_hbm, start),
            )
        )
    ]
    for load in loads:
        load.start()

    barrier = pltpu.get_barrier_semaphore()
    each(
        n - 1,
        lambda r: pl.semaphore_signal(
            barrier, inc=1, device_id=place(partner(n - 1 - r)), device_id_type=pl.DeviceIdType.MESH
        ),
    )
    for load in loads:
        load.wait()

    def beam(b):
        total = None
        for p in range(num_slots):
            term = mm(w[b, p], rf[index_ref[0, b, p]], TN) * live_ref[0, b, p].astype(F32)
            total = term if total is None else total + term
        part[pl.ds(b * width, width), :] = total

    each(num_blocks, beam)
    pl.semaphore_wait(barrier, n - 1)

    def rows_of(d):
        return part.at[pl.ds(pl.multiple_of(d * vox, vox), vox), :]

    def scatter(r):
        d = partner(n - 1 - r)
        send(rows_of(d), slots.at[me], 0, d).start()

    each(n - 1, scatter)
    slots[me] = rows_of(me)[...]
    send(slots.at[pl.ds(0, n - 1)], slots.at[pl.ds(0, n - 1)], 0, me).wait_recv()

    def gather_frame(q):
        if n <= 16:
            total = slots[q]
            for c in range(1, n // n_frame):
                total = total + slots[c * n_frame + q]
            return total
        return lax.fori_loop(1, n // n_frame, lambda c, t: t + slots[c * n_frame + q], slots[q])

    signal = jnp.concatenate([gather_frame(q) for q in range(n_frame)], axis=1)

    s_high, s_low = split(signal)
    t_high, t_low = split(start[...])
    rep_high = jnp.concatenate([s_high] * 4, axis=0)
    rep_low = jnp.concatenate([s_low] * 4, axis=0)
    proj = mm(t_high, rep_high, NT) + mm(t_low, rep_high, NT) + mm(t_high, rep_low, NT)
    p_high = proj.astype(BF16).astype(F32)
    lane = lax.broadcasted_iota(jnp.int32, proj.shape, 1)
    proj = jnp.where(lane < 2 * vox, p_high, proj - p_high).astype(BF16)
    sub_part = mm(proj, jnp.concatenate([s_high, s_low] * 2, axis=0), NN)
    for j in range(n_lane):
        mpart[j] = sub_part[:, j * LANES : (j + 1) * LANES]

    base = (n_chan // 2 - 1) * n_sub * n_frame
    units = n_lane * (RMAX // UNIT)
    reducer = (me >= base) & (me < base + units)

    def unit(ref, u):
        return ref.at[u // (RMAX // UNIT), pl.ds(pl.multiple_of(lax.rem(u, RMAX // UNIT) * UNIT, UNIT), UNIT), :]

    far = jnp.where(me < n // 2, units // 2, 0)

    def to_reducer(r):
        u = lax.rem(far + r, units)

        @pl.when(base + u != me)
        def _():
            send(unit(mpart, u), mslots.at[me], 1, base + u).start()

    each(units, to_reducer)

    @pl.when(reducer)
    def _():
        mine = me - base
        mslots[me] = unit(mpart, mine)[...]
        send(mslots.at[pl.ds(0, n - 1)], mslots.at[pl.ds(0, n - 1)], 1, me).wait_recv()
        if n <= 16:
            total = mslots[0]
            for d in range(1, n):
                total = total + mslots[d]
        else:
            total = lax.fori_loop(1, n, lambda d, t: t + mslots[d], mslots[0])
        unit(full, mine)[...] = total
        each(n - 1, lambda r: send(unit(full, mine), unit(full, mine), 2, partner(n - 1 - r)).start())
        got = mslots.at[pl.ds(0, units - 1)]
        send(got, got, 2, me).wait_recv()

    @pl.when(jnp.logical_not(reducer))
    def _():
        got = mslots.at[pl.ds(0, units)]
        send(got, got, 2, me).wait_recv()

    kept = lax.broadcasted_iota(jnp.int32, (RMAX, 1), 0) < rank_ref[0, 0]
    sub = jnp.concatenate([full[j] for j in range(n_lane)], axis=1)
    sub = jnp.where(kept, sub, 0.0)
    m_high, m_low = split(sub)
    left_high = jnp.concatenate([m_high, s_high], axis=0)
    left_low = jnp.concatenate([m_low, s_low], axis=0)
    rep_high = jnp.concatenate([m_high] * 4, axis=0)
    rep_low = jnp.concatenate([m_low] * 4, axis=0)
    system = mm(left_high, rep_high, NT) + mm(left_low, rep_high, NT) + mm(left_high, rep_low, NT)
    row = lax.broadcasted_iota(jnp.int32, system.shape, 0)
    order = lax.rem(lax.broadcasted_iota(jnp.int32, system.shape, 1), RMAX)
    system = system + jnp.where((row == order) & (row >= rank_ref[0, 0]), 1.0, 0.0)
    order = order[:1]
    for k in range(RMAX):
        at = k % SUBL
        if k and at == 0:
            system = system[SUBL:, :]
        inverse = 1.0 / system[at : at + 1, k : k + 1]
        here = order == k
        factor = jnp.where(here, -inverse, system[at : at + 1, :] * inverse)
        system = jnp.where(here, 0.0, system) - system[:, k : k + 1] * factor
    coeffs = system[SUBL:, :]
    c_high = coeffs.astype(BF16).astype(F32)
    lane = lax.broadcasted_iota(jnp.int32, coeffs.shape, 1)
    coeffs = jnp.where(lane < 2 * RMAX, c_high, coeffs - c_high).astype(BF16)
    clean = signal - mm(coeffs, jnp.concatenate([m_high, m_low] * 2, axis=0), NN)
    power = jnp.sum(clean * clean, axis=1, keepdims=True) * (1.0 / clean.shape[1])
    diagonal = lax.broadcasted_iota(jnp.int32, (vox, vox), 0) == lax.broadcasted_iota(jnp.int32, (vox, vox), 1)
    out_ref[...] = jnp.sum(jnp.where(diagonal, power, 0.0), axis=0, keepdims=True)[None]

    sent = slots.at[pl.ds(0, n - 1)]
    send(sent, sent, 0, me).wait_send()

    @pl.when(reducer)
    def _():
        sent = mslots.at[pl.ds(0, units - 1)]
        send(sent, sent, 1, me).wait_send()
        sent = mslots.at[pl.ds(0, n - 1)]
        send(sent, sent, 2, me).wait_send()

    @pl.when(jnp.logical_not(reducer))
    def _():
        sent = mslots.at[pl.ds(0, units)]
        send(sent, sent, 1, me).wait_send()


def shards(dims, rf, weights, sample_block, live, rank):
    n = math.prod(dims)
    _, num_blocks, num_slots, depth, width = weights.shape
    vox = num_blocks * width // n
    frames = rf.shape[1] * dims[2]
    n_lane = frames // LANES
    rank = rank[None]
    blocks = rf.reshape(rf.shape[0] // depth, depth, rf.shape[1])
    hbm = pl.BlockSpec(memory_space=pl.ANY)
    return pl.pallas_call(
        functools.partial(kernel, dims),
        out_shape=jax.ShapeDtypeStruct((1, 1, vox), F32),
        in_specs=[hbm] * 6,
        out_specs=pl.BlockSpec(memory_space=pltpu.VMEM),
        scratch_shapes=[
            pltpu.SMEM(sample_block.shape, jnp.int32),
            pltpu.SMEM(live.shape, jnp.int32),
            pltpu.SMEM(rank.shape, jnp.int32),
            pltpu.VMEM(blocks.shape, BF16),
            pltpu.VMEM(weights.shape[1:], BF16),
            pltpu.VMEM((RMAX, frames), F32),
            pltpu.VMEM((num_blocks * width, rf.shape[1]), F32),
            pltpu.VMEM((n, vox, rf.shape[1]), F32),
            pltpu.VMEM((n_lane, RMAX, LANES), F32),
            pltpu.VMEM((n, UNIT, LANES), F32),
            pltpu.VMEM((n_lane, RMAX, LANES), F32),
            pltpu.SemaphoreType.DMA((6,)),
            pltpu.SemaphoreType.DMA((3,)),
            pltpu.SemaphoreType.DMA((3,)),
        ],
        compiler_params=pltpu.CompilerParams(
            collective_id=0, has_side_effects=True, vmem_limit_bytes=60 * 1024 * 1024
        ),
        name="power_doppler",
    )(sample_block, live, rank, blocks, weights[0], jnp.asarray(start_basis(frames)))


def solution(mesh):
    dims = (mesh.shape["chan"], mesh.shape["sub"], mesh.shape["frame"])
    return jax.shard_map(
        functools.partial(shards, dims),
        mesh=mesh,
        in_specs=(
            P(("group", "chan", "sub"), "frame"),
            P(("chan", "sub"), None, None, None, None),
            P(("chan", "sub"), None, None),
            P(("chan", "sub"), None, None),
            P("group"),
        ),
        out_specs=P(("group", "chan", "sub"), "frame", None),
        check_vma=False,
    )
```

```python
import functools
import math

import jax
import jax.numpy as jnp
import numpy as np
from jax import lax
from jax.experimental import pallas as pl
from jax.experimental.pallas import tpu as pltpu
from jax.sharding import PartitionSpec as P

RMAX = 32
LANES = 128
SUBL = 8
UNIT = 16
F32 = jnp.float32
BF16 = jnp.bfloat16
NT = (((1,), (1,)), ((), ()))
NN = (((1,), (0,)), ((), ()))
TN = (((0,), (0,)), ((), ()))


def start_basis(frames):
    at = np.arange(frames, dtype=np.float64)[None, :] + 0.5
    order = np.arange(RMAX, dtype=np.float64)[:, None]
    return (np.cos(math.pi * at * order / frames) * math.sqrt(2.0 / frames)).astype(np.float32)


def split(x):
    high = x.astype(BF16)
    return high, (x - high.astype(F32)).astype(BF16)


def mm(a, b, dims):
    return lax.dot_general(a, b, dims, preferred_element_type=F32)


def each(count, body):
    if count <= 16:
        for i in range(count):
            body(i)
    else:
        lax.fori_loop(0, count, lambda i, c: (body(i), c)[1], 0)


def kernel(
    dims,
    index_hbm,
    live_hbm,
    rank_hbm,
    rf_hbm,
    w_hbm,
    start_hbm,
    out_ref,
    index_ref,
    live_ref,
    rank_ref,
    rf,
    w,
    start,
    part,
    slots,
    mpart,
    mslots,
    full,
    load_sem,
    send_sem,
    recv_sem,
):
    n_chan, n_sub, n_frame = dims
    n = n_chan * n_sub * n_frame
    num_blocks, num_slots, depth, width = w.shape
    vox = slots.shape[1]
    n_lane = full.shape[0]
    group = lax.axis_index("group")
    me = (lax.axis_index("chan") * n_sub + lax.axis_index("sub")) * n_frame + lax.axis_index("frame")

    def partner(r):
        if not isinstance(r, int):
            return lax.rem(me + r, n)
        d, bit = me, 1
        while bit <= r:
            if r & bit:
                d = d + bit - 2 * bit * lax.rem(me // bit, 2)
            bit *= 2
        return d

    def place(d):
        return (group, d // (n_sub * n_frame), lax.rem(d, n_frame), lax.rem(d // n_frame, n_sub))

    def send(src, dst, phase, d):
        return pltpu.make_async_remote_copy(
            src_ref=src,
            dst_ref=dst,
            send_sem=send_sem.at[phase],
            recv_sem=recv_sem.at[phase],
            device_id=place(d),
            device_id_type=pl.DeviceIdType.MESH,
        )

    loads = [
        pltpu.make_async_copy(src, dst, load_sem.at[i])
        for i, (src, dst) in enumerate(
            (
                (index_hbm, index_ref),
                (live_hbm, live_ref),
                (rank_hbm, rank_ref),
                (rf_hbm, rf),
                (w_hbm, w),
                (start_hbm, start),
            )
        )
    ]
    for load in loads:
        load.start()

    barrier = pltpu.get_barrier_semaphore()
    each(
        n - 1,
        lambda r: pl.semaphore_signal(
            barrier, inc=1, device_id=place(partner(n - 1 - r)), device_id_type=pl.DeviceIdType.MESH
        ),
    )
    for load in loads:
        load.wait()

    def beam(b):
        total = None
        for p in range(num_slots):
            term = mm(w[b, p], rf[index_ref[0, b, p]], TN) * live_ref[0, b, p].astype(F32)
            total = term if total is None else total + term
        part[pl.ds(b * width, width), :] = total

    each(num_blocks, beam)
    pl.semaphore_wait(barrier, n - 1)

    def rows_of(d):
        return part.at[pl.ds(pl.multiple_of(d * vox, vox), vox), :]

    def scatter(r):
        d = partner(n - 1 - r)
        send(rows_of(d), slots.at[me], 0, d).start()

    each(n - 1, scatter)
    slots[me] = rows_of(me)[...]
    send(slots.at[pl.ds(0, n - 1)], slots.at[pl.ds(0, n - 1)], 0, me).wait_recv()

    def gather_frame(q):
        if n <= 16:
            total = slots[q]
            for c in range(1, n // n_frame):
                total = total + slots[c * n_frame + q]
            return total
        return lax.fori_loop(1, n // n_frame, lambda c, t: t + slots[c * n_frame + q], slots[q])

    signal = jnp.concatenate([gather_frame(q) for q in range(n_frame)], axis=1)

    s_high, s_low = split(signal)
    t_high, t_low = split(start[...])
    rep_high = jnp.concatenate([s_high] * 4, axis=0)
    rep_low = jnp.concatenate([s_low] * 4, axis=0)
    proj = mm(t_high, rep_high, NT) + mm(t_low, rep_high, NT) + mm(t_high, rep_low, NT)
    p_high = proj.astype(BF16).astype(F32)
    lane = lax.broadcasted_iota(jnp.int32, proj.shape, 1)
    proj = jnp.where(lane < 2 * vox, p_high, proj - p_high).astype(BF16)
    sub_part = mm(proj, jnp.concatenate([s_high, s_low] * 2, axis=0), NN)
    for j in range(n_lane):
        mpart[j] = sub_part[:, j * LANES : (j + 1) * LANES]

    base = (n_chan // 2 - 1) * n_sub * n_frame
    units = n_lane * (RMAX // UNIT)
    reducer = (me >= base) & (me < base + units)

    def unit(ref, u):
        return ref.at[u // (RMAX // UNIT), pl.ds(pl.multiple_of(lax.rem(u, RMAX // UNIT) * UNIT, UNIT), UNIT), :]

    far = jnp.where(me < n // 2, units // 2, 0)

    def to_reducer(r):
        u = lax.rem(far + r, units)

        @pl.when(base + u != me)
        def _():
            send(unit(mpart, u), mslots.at[me], 1, base + u).start()

    each(units, to_reducer)

    @pl.when(reducer)
    def _():
        mine = me - base
        mslots[me] = unit(mpart, mine)[...]
        send(mslots.at[pl.ds(0, n - 1)], mslots.at[pl.ds(0, n - 1)], 1, me).wait_recv()
        if n <= 16:
            total = mslots[0]
            for d in range(1, n):
                total = total + mslots[d]
        else:
            total = lax.fori_loop(1, n, lambda d, t: t + mslots[d], mslots[0])
        unit(full, mine)[...] = total
        each(n - 1, lambda r: send(unit(full, mine), unit(full, mine), 2, partner(n - 1 - r)).start())
        got = mslots.at[pl.ds(0, units - 1)]
        send(got, got, 2, me).wait_recv()

    @pl.when(jnp.logical_not(reducer))
    def _():
        got = mslots.at[pl.ds(0, units)]
        send(got, got, 2, me).wait_recv()

    kept = lax.broadcasted_iota(jnp.int32, (RMAX, 1), 0) < rank_ref[0, 0]
    sub = jnp.concatenate([full[j] for j in range(n_lane)], axis=1)
    norm = jnp.sum(sub * sub, axis=1, keepdims=True)
    sub = jnp.where(kept, sub * lax.rsqrt(norm), 0.0)
    m_high, m_low = split(sub)
    left_high = jnp.concatenate([m_high, s_high], axis=0)
    left_low = jnp.concatenate([m_low, s_low], axis=0)
    rep_high = jnp.concatenate([m_high] * 4, axis=0)
    rep_low = jnp.concatenate([m_low] * 4, axis=0)
    system = mm(left_high, rep_high, NT) + mm(left_low, rep_high, NT) + mm(left_high, rep_low, NT)
    row = lax.broadcasted_iota(jnp.int32, system.shape, 0)
    order = lax.rem(lax.broadcasted_iota(jnp.int32, system.shape, 1), RMAX)
    system = system + jnp.where((row == order) & (row >= rank_ref[0, 0]), 1.0, 0.0)
    order = order[:1]
    for k in range(0, RMAX, 2):
        at = k % SUBL
        if k and at == 0:
            system = system[SUBL:, :]
        column0 = jnp.broadcast_to(system[:, k : k + 1], system.shape)
        column1 = jnp.broadcast_to(system[:, k + 1 : k + 2], system.shape)
        here0, here1 = order == k, order == k + 1
        row0 = jnp.where(here0, -1.0, jnp.where(here1, 0.0, system[at : at + 1, :]))
        row1 = jnp.where(here0, 0.0, jnp.where(here1, -1.0, system[at + 1 : at + 2, :]))
        p00, p01, p11 = column0[at : at + 1, :], column1[at : at + 1, :], column1[at + 1 : at + 2, :]
        inverse = 1.0 / (p00 * p11 - p01 * p01)
        factor0 = (p11 * row0 - p01 * row1) * inverse
        factor1 = (p00 * row1 - p01 * row0) * inverse
        system = jnp.where(here0 | here1, 0.0, system) - column0 * factor0 - column1 * factor1
    coeffs = system[SUBL:, :]
    c_high = coeffs.astype(BF16).astype(F32)
    lane = lax.broadcasted_iota(jnp.int32, coeffs.shape, 1)
    coeffs = jnp.where(lane < 2 * RMAX, c_high, coeffs - c_high).astype(BF16)
    clean = signal - mm(coeffs, jnp.concatenate([m_high, m_low] * 2, axis=0), NN)
    power = jnp.sum(clean * clean, axis=1, keepdims=True) * (1.0 / clean.shape[1])
    diagonal = lax.broadcasted_iota(jnp.int32, (vox, vox), 0) == lax.broadcasted_iota(jnp.int32, (vox, vox), 1)
    out_ref[...] = jnp.sum(jnp.where(diagonal, power, 0.0), axis=0, keepdims=True)[None]

    sent = slots.at[pl.ds(0, n - 1)]
    send(sent, sent, 0, me).wait_send()

    @pl.when(reducer)
    def _():
        sent = mslots.at[pl.ds(0, units - 1)]
        send(sent, sent, 1, me).wait_send()
        sent = mslots.at[pl.ds(0, n - 1)]
        send(sent, sent, 2, me).wait_send()

    @pl.when(jnp.logical_not(reducer))
    def _():
        sent = mslots.at[pl.ds(0, units)]
        send(sent, sent, 1, me).wait_send()


def shards(dims, rf, weights, sample_block, live, rank):
    n = math.prod(dims)
    _, num_blocks, num_slots, depth, width = weights.shape
    vox = num_blocks * width // n
    frames = rf.shape[1] * dims[2]
    n_lane = frames // LANES
    rank = rank[None]
    blocks = rf.reshape(rf.shape[0] // depth, depth, rf.shape[1])
    hbm = pl.BlockSpec(memory_space=pl.ANY)
    return pl.pallas_call(
        functools.partial(kernel, dims),
        out_shape=pltpu.VMEM((1, 1, vox), F32),
        in_specs=[hbm] * 6,
        out_specs=pl.BlockSpec(memory_space=pltpu.VMEM),
        scratch_shapes=[
            pltpu.SMEM(sample_block.shape, jnp.int32),
            pltpu.SMEM(live.shape, jnp.int32),
            pltpu.SMEM(rank.shape, jnp.int32),
            pltpu.VMEM(blocks.shape, BF16),
            pltpu.VMEM(weights.shape[1:], BF16),
            pltpu.VMEM((RMAX, frames), F32),
            pltpu.VMEM((num_blocks * width, rf.shape[1]), F32),
            pltpu.VMEM((n, vox, rf.shape[1]), F32),
            pltpu.VMEM((n_lane, RMAX, LANES), F32),
            pltpu.VMEM((n, UNIT, LANES), F32),
            pltpu.VMEM((n_lane, RMAX, LANES), F32),
            pltpu.SemaphoreType.DMA((6,)),
            pltpu.SemaphoreType.DMA((3,)),
            pltpu.SemaphoreType.DMA((3,)),
        ],
        compiler_params=pltpu.CompilerParams(
            collective_id=0, has_side_effects=True, vmem_limit_bytes=60 * 1024 * 1024
        ),
        name="power_doppler",
    )(sample_block, live, rank, blocks, weights[0], jnp.asarray(start_basis(frames)))


def solution(mesh):
    dims = (mesh.shape["chan"], mesh.shape["sub"], mesh.shape["frame"])
    return jax.shard_map(
        functools.partial(shards, dims),
        mesh=mesh,
        in_specs=(
            P(("group", "chan", "sub"), "frame"),
            P(("chan", "sub"), None, None, None, None),
            P(("chan", "sub"), None, None),
            P(("chan", "sub"), None, None),
            P("group"),
        ),
        out_specs=P(("group", "chan", "sub"), "frame", None),
        check_vma=False,
    )
```

```python
import functools
import math

import jax
import jax.numpy as jnp
import numpy as np
from jax import lax
from jax.experimental import pallas as pl
from jax.experimental.pallas import tpu as pltpu
from jax.sharding import PartitionSpec as P

RMAX = 32
LANES = 128
SUBL = 8
UNIT = 16
F32 = jnp.float32
BF16 = jnp.bfloat16
NT = (((1,), (1,)), ((), ()))
NN = (((1,), (0,)), ((), ()))
TN = (((0,), (0,)), ((), ()))


def start_basis(frames):
    at = np.arange(frames, dtype=np.float64)[None, :] + 0.5
    order = np.arange(RMAX, dtype=np.float64)[:, None]
    return (np.cos(math.pi * at * order / frames) * math.sqrt(2.0 / frames)).astype(np.float32)


def split(x):
    high = x.astype(BF16)
    return high, (x - high.astype(F32)).astype(BF16)


def mm(a, b, dims):
    return lax.dot_general(a, b, dims, preferred_element_type=F32)


def each(count, body):
    if count <= 16:
        for i in range(count):
            body(i)
    else:
        lax.fori_loop(0, count, lambda i, c: (body(i), c)[1], 0)


def kernel(
    dims,
    index_hbm,
    live_hbm,
    rank_hbm,
    rf_hbm,
    w_hbm,
    start_hbm,
    out_ref,
    index_ref,
    live_ref,
    rank_ref,
    rf,
    w,
    start,
    part,
    pair,
    sums,
    slots,
    mpart,
    mslots,
    full,
    load_sem,
    send_sem,
    recv_sem,
    pair_send,
    pair_recv,
):
    n_chan, n_sub, n_frame = dims
    n = n_chan * n_sub * n_frame
    num_blocks, num_slots, depth, width = w.shape
    vox = slots.shape[1]
    n_lane = full.shape[0]
    group = lax.axis_index("group")
    me = (lax.axis_index("chan") * n_sub + lax.axis_index("sub")) * n_frame + lax.axis_index("frame")

    def partner(r):
        if not isinstance(r, int):
            return lax.rem(me + r, n)
        d, bit = me, 1
        while bit <= r:
            if r & bit:
                d = d + bit - 2 * bit * lax.rem(me // bit, 2)
            bit *= 2
        return d

    def place(d):
        return (group, d // (n_sub * n_frame), lax.rem(d, n_frame), lax.rem(d // n_frame, n_sub))

    def send(src, dst, phase, d):
        return pltpu.make_async_remote_copy(
            src_ref=src,
            dst_ref=dst,
            send_sem=send_sem.at[phase],
            recv_sem=recv_sem.at[phase],
            device_id=place(d),
            device_id_type=pl.DeviceIdType.MESH,
        )

    loads = [
        pltpu.make_async_copy(src, dst, load_sem.at[i])
        for i, (src, dst) in enumerate(
            (
                (index_hbm, index_ref),
                (live_hbm, live_ref),
                (rank_hbm, rank_ref),
                (rf_hbm, rf),
                (w_hbm, w),
                (start_hbm, start),
            )
        )
    ]
    for load in loads:
        load.start()

    barrier = pltpu.get_barrier_semaphore()
    each(
        n - 1,
        lambda r: pl.semaphore_signal(
            barrier, inc=1, device_id=place(partner(n - 1 - r)), device_id_type=pl.DeviceIdType.MESH
        ),
    )
    for load in loads:
        load.wait()

    def beam(b):
        total = None
        for p in range(num_slots):
            term = mm(w[b, p], rf[index_ref[0, b, p]], TN) * live_ref[0, b, p].astype(F32)
            total = term if total is None else total + term
        part[pl.ds(b * width, width), :] = total

    each(num_blocks, beam)
    pl.semaphore_wait(barrier, n - 1)

    sub, frame = lax.axis_index("sub"), lax.axis_index("frame")
    chan = lax.axis_index("chan")
    span = n_frame * vox

    def rows(c, s):
        return pl.ds(pl.multiple_of((c * n_sub + s) * span, span), span)

    def nth_chan(r):
        if n_chan <= 4:
            c, bit = chan, 1
            flip = n_chan - 1 - r
            while bit <= flip:
                if flip & bit:
                    c = c + bit - 2 * bit * lax.rem(chan // bit, 2)
                bit *= 2
            return c
        return lax.rem(chan + r + 1, n_chan)

    def exchange(r):
        c = nth_chan(r)
        return pltpu.make_async_remote_copy(
            src_ref=part.at[rows(c, 1 - sub), :],
            dst_ref=pair.at[r],
            send_sem=pair_send.at[r],
            recv_sem=pair_recv.at[r],
            device_id=(group, chan, frame, 1 - sub),
            device_id_type=pl.DeviceIdType.MESH,
        )

    each(n_chan, lambda r: exchange(r).start())
    mine = chan * n_frame + frame

    def scatter(r):
        c = nth_chan(r)
        exchange(r).wait_recv()
        sums[r] = pair[r] + part[rows(c, sub), :]
        for step in range(n_frame):
            q = lax.rem(frame + n_frame - 1 - step, n_frame)
            source = sums.at[r, pl.ds(pl.multiple_of(q * vox, vox), vox), :]

            def go():
                send(source, slots.at[mine], 0, (c * n_sub + sub) * n_frame + q).start()

            if n_chan <= 4 and r < n_chan - 1 or step < n_frame - 1:
                go()
            elif n_chan <= 4:
                slots[mine] = source[...]
            else:
                pl.when(r < n_chan - 1)(go)

    each(n_chan, scatter)
    if n_chan > 4:
        slots[mine] = sums[n_chan - 1, pl.ds(pl.multiple_of(frame * vox, vox), vox), :]
    peers = n_chan * n_frame
    got = slots.at[pl.ds(0, peers - 1)]
    send(got, got, 0, me).wait_recv()

    def gather_frame(q):
        if n <= 16:
            total = slots[q]
            for c in range(1, n_chan):
                total = total + slots[c * n_frame + q]
            return total
        return lax.fori_loop(1, n_chan, lambda c, t: t + slots[c * n_frame + q], slots[q])

    signal = jnp.concatenate([gather_frame(q) for q in range(n_frame)], axis=1)

    s_high, s_low = split(signal)
    t_high, t_low = split(start[...])
    rep_high = jnp.concatenate([s_high] * 4, axis=0)
    rep_low = jnp.concatenate([s_low] * 4, axis=0)
    proj = mm(t_high, rep_high, NT) + mm(t_low, rep_high, NT) + mm(t_high, rep_low, NT)
    p_high = proj.astype(BF16).astype(F32)
    lane = lax.broadcasted_iota(jnp.int32, proj.shape, 1)
    proj = jnp.where(lane < 2 * vox, p_high, proj - p_high).astype(BF16)
    sub_part = mm(proj, jnp.concatenate([s_high, s_low] * 2, axis=0), NN)
    for j in range(n_lane):
        mpart[j] = sub_part[:, j * LANES : (j + 1) * LANES]

    base = (n_chan // 2 - 1) * n_sub * n_frame
    units = n_lane * (RMAX // UNIT)
    reducer = (me >= base) & (me < base + units)

    def unit(ref, u):
        return ref.at[u // (RMAX // UNIT), pl.ds(pl.multiple_of(lax.rem(u, RMAX // UNIT) * UNIT, UNIT), UNIT), :]

    far = jnp.where(me < n // 2, units // 2, 0)

    def to_reducer(r):
        u = lax.rem(far + r, units)

        @pl.when(base + u != me)
        def _():
            send(unit(mpart, u), mslots.at[me], 1, base + u).start()

    each(units, to_reducer)

    @pl.when(reducer)
    def _():
        mine = me - base
        mslots[me] = unit(mpart, mine)[...]
        send(mslots.at[pl.ds(0, n - 1)], mslots.at[pl.ds(0, n - 1)], 1, me).wait_recv()
        if n <= 16:
            total = mslots[0]
            for d in range(1, n):
                total = total + mslots[d]
        else:
            total = lax.fori_loop(1, n, lambda d, t: t + mslots[d], mslots[0])
        unit(full, mine)[...] = total
        each(n - 1, lambda r: send(unit(full, mine), unit(full, mine), 2, partner(n - 1 - r)).start())
        got = mslots.at[pl.ds(0, units - 1)]
        send(got, got, 2, me).wait_recv()

    @pl.when(jnp.logical_not(reducer))
    def _():
        got = mslots.at[pl.ds(0, units)]
        send(got, got, 2, me).wait_recv()

    kept = lax.broadcasted_iota(jnp.int32, (RMAX, 1), 0) < rank_ref[0, 0]
    space = jnp.concatenate([full[j] for j in range(n_lane)], axis=1)
    norm = jnp.sum(space * space, axis=1, keepdims=True)
    space = jnp.where(kept, space * lax.rsqrt(norm), 0.0)
    m_high, m_low = split(space)
    left_high = jnp.concatenate([m_high, s_high], axis=0)
    left_low = jnp.concatenate([m_low, s_low], axis=0)
    rep_high = jnp.concatenate([m_high] * 4, axis=0)
    rep_low = jnp.concatenate([m_low] * 4, axis=0)
    system = mm(left_high, rep_high, NT) + mm(left_low, rep_high, NT) + mm(left_high, rep_low, NT)
    row = lax.broadcasted_iota(jnp.int32, system.shape, 0)
    order = lax.rem(lax.broadcasted_iota(jnp.int32, system.shape, 1), RMAX)
    system = system + jnp.where((row == order) & (row >= rank_ref[0, 0]), 1.0, 0.0)
    order = order[:1]
    for k in range(0, RMAX, 2):
        at = k % SUBL
        if k and at == 0:
            system = system[SUBL:, :]
        column0 = jnp.broadcast_to(system[:, k : k + 1], system.shape)
        column1 = jnp.broadcast_to(system[:, k + 1 : k + 2], system.shape)
        here0, here1 = order == k, order == k + 1
        row0 = jnp.where(here0, -1.0, jnp.where(here1, 0.0, system[at : at + 1, :]))
        row1 = jnp.where(here0, 0.0, jnp.where(here1, -1.0, system[at + 1 : at + 2, :]))
        p00, p01, p11 = column0[at : at + 1, :], column1[at : at + 1, :], column1[at + 1 : at + 2, :]
        inverse = 1.0 / (p00 * p11 - p01 * p01)
        factor0 = (p11 * row0 - p01 * row1) * inverse
        factor1 = (p00 * row1 - p01 * row0) * inverse
        system = jnp.where(here0 | here1, 0.0, system) - column0 * factor0 - column1 * factor1
    coeffs = system[SUBL:, :]
    c_high = coeffs.astype(BF16).astype(F32)
    lane = lax.broadcasted_iota(jnp.int32, coeffs.shape, 1)
    coeffs = jnp.where(lane < 2 * RMAX, c_high, coeffs - c_high).astype(BF16)
    clean = signal - mm(coeffs, jnp.concatenate([m_high, m_low] * 2, axis=0), NN)
    power = jnp.sum(clean * clean, axis=1, keepdims=True) * (1.0 / clean.shape[1])
    diagonal = lax.broadcasted_iota(jnp.int32, (vox, vox), 0) == lax.broadcasted_iota(jnp.int32, (vox, vox), 1)
    out_ref[...] = jnp.sum(jnp.where(diagonal, power, 0.0), axis=0, keepdims=True)[None]

    sent = slots.at[pl.ds(0, peers - 1)]
    send(sent, sent, 0, me).wait_send()
    each(n_chan, lambda r: exchange(r).wait_send())

    @pl.when(reducer)
    def _():
        sent = mslots.at[pl.ds(0, units - 1)]
        send(sent, sent, 1, me).wait_send()
        sent = mslots.at[pl.ds(0, n - 1)]
        send(sent, sent, 2, me).wait_send()

    @pl.when(jnp.logical_not(reducer))
    def _():
        sent = mslots.at[pl.ds(0, units)]
        send(sent, sent, 1, me).wait_send()


def shards(dims, rf, weights, sample_block, live, rank):
    n = math.prod(dims)
    _, num_blocks, num_slots, depth, width = weights.shape
    vox = num_blocks * width // n
    frames = rf.shape[1] * dims[2]
    n_lane = frames // LANES
    rank = rank[None]
    blocks = rf.reshape(rf.shape[0] // depth, depth, rf.shape[1])
    hbm = pl.BlockSpec(memory_space=pl.ANY)
    return pl.pallas_call(
        functools.partial(kernel, dims),
        out_shape=pltpu.VMEM((1, 1, vox), F32),
        in_specs=[hbm] * 6,
        out_specs=pl.BlockSpec(memory_space=pltpu.VMEM),
        scratch_shapes=[
            pltpu.SMEM(sample_block.shape, jnp.int32),
            pltpu.SMEM(live.shape, jnp.int32),
            pltpu.SMEM(rank.shape, jnp.int32),
            pltpu.VMEM(blocks.shape, BF16),
            pltpu.VMEM(weights.shape[1:], BF16),
            pltpu.VMEM((RMAX, frames), F32),
            pltpu.VMEM((num_blocks * width, rf.shape[1]), F32),
            pltpu.VMEM((dims[0], dims[2] * vox, rf.shape[1]), F32),
            pltpu.VMEM((dims[0], dims[2] * vox, rf.shape[1]), F32),
            pltpu.VMEM((dims[0] * dims[2], vox, rf.shape[1]), F32),
            pltpu.VMEM((n_lane, RMAX, LANES), F32),
            pltpu.VMEM((n, UNIT, LANES), F32),
            pltpu.VMEM((n_lane, RMAX, LANES), F32),
            pltpu.SemaphoreType.DMA((6,)),
            pltpu.SemaphoreType.DMA((3,)),
            pltpu.SemaphoreType.DMA((3,)),
            pltpu.SemaphoreType.DMA((dims[0],)),
            pltpu.SemaphoreType.DMA((dims[0],)),
        ],
        compiler_params=pltpu.CompilerParams(
            collective_id=0, has_side_effects=True, vmem_limit_bytes=60 * 1024 * 1024
        ),
        name="power_doppler",
    )(sample_block, live, rank, blocks, weights[0], jnp.asarray(start_basis(frames)))


def solution(mesh):
    dims = (mesh.shape["chan"], mesh.shape["sub"], mesh.shape["frame"])
    return jax.shard_map(
        functools.partial(shards, dims),
        mesh=mesh,
        in_specs=(
            P(("group", "chan", "sub"), "frame"),
            P(("chan", "sub"), None, None, None, None),
            P(("chan", "sub"), None, None),
            P(("chan", "sub"), None, None),
            P("group"),
        ),
        out_specs=P(("group", "chan", "sub"), "frame", None),
        check_vma=False,
    )
```

```python
import functools
import math

import jax
import jax.numpy as jnp
import numpy as np
from jax import lax
from jax.experimental import pallas as pl
from jax.experimental.pallas import tpu as pltpu
from jax.sharding import PartitionSpec as P

RMAX = 32
LANES = 128
SUBL = 8
UNIT = 16
F32 = jnp.float32
BF16 = jnp.bfloat16
NT = (((1,), (1,)), ((), ()))
NN = (((1,), (0,)), ((), ()))
TN = (((0,), (0,)), ((), ()))


def start_basis(frames):
    at = np.arange(frames, dtype=np.float64)[None, :] + 0.5
    order = np.arange(RMAX, dtype=np.float64)[:, None]
    return (np.cos(math.pi * at * order / frames) * math.sqrt(2.0 / frames)).astype(np.float32)


def split(x):
    high = x.astype(BF16)
    return high, (x - high.astype(F32)).astype(BF16)


def mm(a, b, dims):
    return lax.dot_general(a, b, dims, preferred_element_type=F32)


def each(count, body):
    if count <= 16:
        for i in range(count):
            body(i)
    else:
        lax.fori_loop(0, count, lambda i, c: (body(i), c)[1], 0)


def kernel(
    dims,
    index_hbm,
    live_hbm,
    rank_hbm,
    rf_hbm,
    w_hbm,
    start_hbm,
    out_ref,
    index_ref,
    live_ref,
    rank_ref,
    rf,
    w,
    start,
    part,
    pair,
    sums,
    slots,
    mpart,
    mslots,
    full,
    load_sem,
    send_sem,
    recv_sem,
    pair_send,
    pair_recv,
):
    n_chan, n_sub, n_frame = dims
    n = n_chan * n_sub * n_frame
    num_blocks, num_slots, depth, width = w.shape
    vox = slots.shape[1]
    n_lane = full.shape[0]
    group = lax.axis_index("group")
    me = (lax.axis_index("chan") * n_sub + lax.axis_index("sub")) * n_frame + lax.axis_index("frame")

    def partner(r):
        if not isinstance(r, int):
            return lax.rem(me + r, n)
        d, bit = me, 1
        while bit <= r:
            if r & bit:
                d = d + bit - 2 * bit * lax.rem(me // bit, 2)
            bit *= 2
        return d

    def place(d):
        return (group, d // (n_sub * n_frame), lax.rem(d, n_frame), lax.rem(d // n_frame, n_sub))

    def send(src, dst, phase, d):
        return pltpu.make_async_remote_copy(
            src_ref=src,
            dst_ref=dst,
            send_sem=send_sem.at[phase],
            recv_sem=recv_sem.at[phase],
            device_id=place(d),
            device_id_type=pl.DeviceIdType.MESH,
        )

    loads = [
        pltpu.make_async_copy(src, dst, load_sem.at[i])
        for i, (src, dst) in enumerate(
            (
                (index_hbm, index_ref),
                (live_hbm, live_ref),
                (rank_hbm, rank_ref),
                (rf_hbm, rf),
                (w_hbm, w),
                (start_hbm, start),
            )
        )
    ]
    barrier = pltpu.get_barrier_semaphore()
    each(
        n - 1,
        lambda r: pl.semaphore_signal(
            barrier, inc=1, device_id=place(partner(n - 1 - r)), device_id_type=pl.DeviceIdType.MESH
        ),
    )
    for load in loads:
        load.start()
    for load in loads:
        load.wait()

    def beam(b):
        total = None
        for p in range(num_slots):
            term = mm(w[b, p], rf[index_ref[0, b, p]], TN) * live_ref[0, b, p].astype(F32)
            total = term if total is None else total + term
        part[pl.ds(b * width, width), :] = total

    each(num_blocks, beam)
    pl.semaphore_wait(barrier, n - 1)

    sub, frame = lax.axis_index("sub"), lax.axis_index("frame")
    chan = lax.axis_index("chan")
    span = n_frame * vox

    def rows(c, s):
        return pl.ds(pl.multiple_of((c * n_sub + s) * span, span), span)

    def nth_chan(r):
        if n_chan <= 4:
            c, bit = chan, 1
            flip = n_chan - 1 - r
            while bit <= flip:
                if flip & bit:
                    c = c + bit - 2 * bit * lax.rem(chan // bit, 2)
                bit *= 2
            return c
        return lax.rem(chan + r + 1, n_chan)

    def exchange(r):
        c = nth_chan(r)
        return pltpu.make_async_remote_copy(
            src_ref=part.at[rows(c, 1 - sub), :],
            dst_ref=pair.at[r],
            send_sem=pair_send.at[r],
            recv_sem=pair_recv.at[r],
            device_id=(group, chan, frame, 1 - sub),
            device_id_type=pl.DeviceIdType.MESH,
        )

    each(n_chan, lambda r: exchange(r).start())
    mine = chan * n_frame + frame

    def scatter(r):
        c = nth_chan(r)
        exchange(r).wait_recv()
        sums[r] = pair[r] + part[rows(c, sub), :]
        for step in range(n_frame):
            q = lax.rem(frame + n_frame - 1 - step, n_frame)
            source = sums.at[r, pl.ds(pl.multiple_of(q * vox, vox), vox), :]

            def go():
                send(source, slots.at[mine], 0, (c * n_sub + sub) * n_frame + q).start()

            if n_chan <= 4 and r < n_chan - 1 or step < n_frame - 1:
                go()
            elif n_chan <= 4:
                slots[mine] = source[...]
            else:
                pl.when(r < n_chan - 1)(go)

    each(n_chan, scatter)
    if n_chan > 4:
        slots[mine] = sums[n_chan - 1, pl.ds(pl.multiple_of(frame * vox, vox), vox), :]
    peers = n_chan * n_frame
    got = slots.at[pl.ds(0, peers - 1)]
    send(got, got, 0, me).wait_recv()

    def gather_frame(q):
        if n <= 16:
            total = slots[q]
            for c in range(1, n_chan):
                total = total + slots[c * n_frame + q]
            return total
        return lax.fori_loop(1, n_chan, lambda c, t: t + slots[c * n_frame + q], slots[q])

    signal = jnp.concatenate([gather_frame(q) for q in range(n_frame)], axis=1)

    s_high, s_low = split(signal)
    t_high, t_low = split(start[...])
    rep_high = jnp.concatenate([s_high] * 4, axis=0)
    rep_low = jnp.concatenate([s_low] * 4, axis=0)
    proj = mm(t_high, rep_high, NT) + mm(t_low, rep_high, NT) + mm(t_high, rep_low, NT)
    p_high = proj.astype(BF16).astype(F32)
    lane = lax.broadcasted_iota(jnp.int32, proj.shape, 1)
    proj = jnp.where(lane < 2 * vox, p_high, proj - p_high).astype(BF16)
    sub_part = mm(proj, jnp.concatenate([s_high, s_low] * 2, axis=0), NN)
    for j in range(n_lane):
        mpart[j] = sub_part[:, j * LANES : (j + 1) * LANES]

    base = (n_chan // 2 - 1) * n_sub * n_frame
    units = n_lane * (RMAX // UNIT)
    reducer = (me >= base) & (me < base + units)

    def unit(ref, u):
        return ref.at[u // (RMAX // UNIT), pl.ds(pl.multiple_of(lax.rem(u, RMAX // UNIT) * UNIT, UNIT), UNIT), :]

    far = jnp.where(me < n // 2, units // 2, 0)

    def to_reducer(r):
        u = lax.rem(far + r, units)

        @pl.when(base + u != me)
        def _():
            send(unit(mpart, u), mslots.at[me], 1, base + u).start()

    each(units, to_reducer)

    @pl.when(reducer)
    def _():
        mine = me - base
        mslots[me] = unit(mpart, mine)[...]
        send(mslots.at[pl.ds(0, n - 1)], mslots.at[pl.ds(0, n - 1)], 1, me).wait_recv()
        if n <= 16:
            total = mslots[0]
            for d in range(1, n):
                total = total + mslots[d]
        else:
            total = lax.fori_loop(1, n, lambda d, t: t + mslots[d], mslots[0])
        unit(full, mine)[...] = total
        each(n - 1, lambda r: send(unit(full, mine), unit(full, mine), 2, partner(n - 1 - r)).start())
        got = mslots.at[pl.ds(0, units - 1)]
        send(got, got, 2, me).wait_recv()

    @pl.when(jnp.logical_not(reducer))
    def _():
        got = mslots.at[pl.ds(0, units)]
        send(got, got, 2, me).wait_recv()

    kept = lax.broadcasted_iota(jnp.int32, (RMAX, 1), 0) < rank_ref[0, 0]
    space = jnp.concatenate([full[j] for j in range(n_lane)], axis=1)
    norm = jnp.sum(space * space, axis=1, keepdims=True)
    space = jnp.where(kept, space * lax.rsqrt(norm), 0.0)
    m_high, m_low = split(space)
    left_high = jnp.concatenate([m_high, s_high], axis=0)
    left_low = jnp.concatenate([m_low, s_low], axis=0)
    rep_high = jnp.concatenate([m_high] * 4, axis=0)
    rep_low = jnp.concatenate([m_low] * 4, axis=0)
    system = mm(left_high, rep_high, NT) + mm(left_low, rep_high, NT) + mm(left_high, rep_low, NT)
    row = lax.broadcasted_iota(jnp.int32, system.shape, 0)
    order = lax.rem(lax.broadcasted_iota(jnp.int32, system.shape, 1), RMAX)
    system = system + jnp.where((row == order) & (row >= rank_ref[0, 0]), 1.0, 0.0)
    order = order[:1]
    for panel in range(0, RMAX, SUBL):
        if panel:
            system = system[SUBL:, :]
        columns = [jnp.broadcast_to(system[:, panel + i : panel + i + 1], system.shape) for i in range(SUBL)]
        for i in range(0, SUBL, 2):
            column0, column1 = columns[i : i + 2]
            p00, p01, p11 = column0[i : i + 1, :], column1[i : i + 1, :], column1[i + 1 : i + 2, :]
            inverse = 1.0 / (p00 * p11 - p01 * p01)

            def update(target, row0, row1):
                factor0 = (p11 * row0 - p01 * row1) * inverse
                factor1 = (p00 * row1 - p01 * row0) * inverse
                return target - column0 * factor0 - column1 * factor1

            for j in range(i + 2, SUBL):
                columns[j] = update(columns[j], columns[j][i : i + 1, :], columns[j][i + 1 : i + 2, :])
            here0, here1 = order == panel + i, order == panel + i + 1
            row0 = jnp.where(here0, -1.0, jnp.where(here1, 0.0, system[i : i + 1, :]))
            row1 = jnp.where(here0, 0.0, jnp.where(here1, -1.0, system[i + 1 : i + 2, :]))
            system = update(jnp.where(here0 | here1, 0.0, system), row0, row1)
    coeffs = system[SUBL:, :]
    c_high = coeffs.astype(BF16).astype(F32)
    lane = lax.broadcasted_iota(jnp.int32, coeffs.shape, 1)
    coeffs = jnp.where(lane < 2 * RMAX, c_high, coeffs - c_high).astype(BF16)
    clean = signal - mm(coeffs, jnp.concatenate([m_high, m_low] * 2, axis=0), NN)
    power = jnp.sum(clean * clean, axis=1, keepdims=True) * (1.0 / clean.shape[1])
    diagonal = lax.broadcasted_iota(jnp.int32, (vox, vox), 0) == lax.broadcasted_iota(jnp.int32, (vox, vox), 1)
    out_ref[...] = jnp.sum(jnp.where(diagonal, power, 0.0), axis=0, keepdims=True)[None]

    sent = slots.at[pl.ds(0, peers - 1)]
    send(sent, sent, 0, me).wait_send()
    each(n_chan, lambda r: exchange(r).wait_send())

    @pl.when(reducer)
    def _():
        sent = mslots.at[pl.ds(0, units - 1)]
        send(sent, sent, 1, me).wait_send()
        sent = mslots.at[pl.ds(0, n - 1)]
        send(sent, sent, 2, me).wait_send()

    @pl.when(jnp.logical_not(reducer))
    def _():
        sent = mslots.at[pl.ds(0, units)]
        send(sent, sent, 1, me).wait_send()


def shards(dims, rf, weights, sample_block, live, rank):
    n = math.prod(dims)
    _, num_blocks, num_slots, depth, width = weights.shape
    vox = num_blocks * width // n
    frames = rf.shape[1] * dims[2]
    n_lane = frames // LANES
    rank = rank[None]
    blocks = rf.reshape(rf.shape[0] // depth, depth, rf.shape[1])
    hbm = pl.BlockSpec(memory_space=pl.ANY)
    return pl.pallas_call(
        functools.partial(kernel, dims),
        out_shape=pltpu.VMEM((1, 1, vox), F32),
        in_specs=[hbm] * 6,
        out_specs=pl.BlockSpec(memory_space=pltpu.VMEM),
        scratch_shapes=[
            pltpu.SMEM(sample_block.shape, jnp.int32),
            pltpu.SMEM(live.shape, jnp.int32),
            pltpu.SMEM(rank.shape, jnp.int32),
            pltpu.VMEM(blocks.shape, BF16),
            pltpu.VMEM(weights.shape[1:], BF16),
            pltpu.VMEM((RMAX, frames), F32),
            pltpu.VMEM((num_blocks * width, rf.shape[1]), F32),
            pltpu.VMEM((dims[0], dims[2] * vox, rf.shape[1]), F32),
            pltpu.VMEM((dims[0], dims[2] * vox, rf.shape[1]), F32),
            pltpu.VMEM((dims[0] * dims[2], vox, rf.shape[1]), F32),
            pltpu.VMEM((n_lane, RMAX, LANES), F32),
            pltpu.VMEM((n, UNIT, LANES), F32),
            pltpu.VMEM((n_lane, RMAX, LANES), F32),
            pltpu.SemaphoreType.DMA((6,)),
            pltpu.SemaphoreType.DMA((3,)),
            pltpu.SemaphoreType.DMA((3,)),
            pltpu.SemaphoreType.DMA((dims[0],)),
            pltpu.SemaphoreType.DMA((dims[0],)),
        ],
        compiler_params=pltpu.CompilerParams(
            collective_id=0, has_side_effects=True, vmem_limit_bytes=60 * 1024 * 1024
        ),
        name="power_doppler",
    )(sample_block, live, rank, blocks, weights[0], jnp.asarray(start_basis(frames)))


def solution(mesh):
    dims = (mesh.shape["chan"], mesh.shape["sub"], mesh.shape["frame"])
    return jax.shard_map(
        functools.partial(shards, dims),
        mesh=mesh,
        in_specs=(
            P(("group", "chan", "sub"), "frame"),
            P(("chan", "sub"), None, None, None, None),
            P(("chan", "sub"), None, None),
            P(("chan", "sub"), None, None),
            P("group"),
        ),
        out_specs=P(("group", "chan", "sub"), "frame", None),
        check_vma=False,
    )
```

```python
import functools
import math

import jax
import jax.numpy as jnp
import numpy as np
from jax import lax
from jax.experimental import pallas as pl
from jax.experimental.pallas import tpu as pltpu
from jax.sharding import PartitionSpec as P

RMAX = 32
LANES = 128
SUBL = 8
UNIT = 16
F32 = jnp.float32
BF16 = jnp.bfloat16
NT = (((1,), (1,)), ((), ()))
NN = (((1,), (0,)), ((), ()))
TN = (((0,), (0,)), ((), ()))


def start_basis(frames):
    at = np.arange(frames, dtype=np.float64)[None, :] + 0.5
    order = np.arange(RMAX, dtype=np.float64)[:, None]
    return (np.cos(math.pi * at * order / frames) * math.sqrt(2.0 / frames)).astype(np.float32)


def split(x):
    high = x.astype(BF16)
    return high, (x - high.astype(F32)).astype(BF16)


def mm(a, b, dims):
    return lax.dot_general(a, b, dims, preferred_element_type=F32)


def each(count, body):
    if count <= 16:
        for i in range(count):
            body(i)
    else:
        lax.fori_loop(0, count, lambda i, c: (body(i), c)[1], 0)


def kernel(
    dims,
    index_hbm,
    live_hbm,
    rank_hbm,
    rf_hbm,
    w_hbm,
    start_hbm,
    out_ref,
    index_ref,
    live_ref,
    rank_ref,
    rf,
    w,
    start,
    part,
    pair,
    sums,
    slots,
    mpart,
    mslots,
    full,
    load_sem,
    send_sem,
    recv_sem,
    pair_send,
    pair_recv,
):
    n_chan, n_sub, n_frame = dims
    n = n_chan * n_sub * n_frame
    num_blocks, num_slots, depth, width = w.shape
    vox = slots.shape[1]
    n_lane = full.shape[0]
    group = lax.axis_index("group")
    me = (lax.axis_index("chan") * n_sub + lax.axis_index("sub")) * n_frame + lax.axis_index("frame")

    def partner(r):
        if not isinstance(r, int):
            return lax.rem(me + r, n)
        d, bit = me, 1
        while bit <= r:
            if r & bit:
                d = d + bit - 2 * bit * lax.rem(me // bit, 2)
            bit *= 2
        return d

    def place(d):
        return (group, d // (n_sub * n_frame), lax.rem(d, n_frame), lax.rem(d // n_frame, n_sub))

    def send(src, dst, phase, d):
        return pltpu.make_async_remote_copy(
            src_ref=src,
            dst_ref=dst,
            send_sem=send_sem.at[phase],
            recv_sem=recv_sem.at[phase],
            device_id=place(d),
            device_id_type=pl.DeviceIdType.MESH,
        )

    loads = [
        pltpu.make_async_copy(src, dst, load_sem.at[i])
        for i, (src, dst) in enumerate(
            (
                (index_hbm, index_ref),
                (live_hbm, live_ref),
                (rank_hbm, rank_ref),
                (rf_hbm, rf),
                (w_hbm, w),
                (start_hbm, start),
            )
        )
    ]
    barrier = pltpu.get_barrier_semaphore()
    each(
        n - 1,
        lambda r: pl.semaphore_signal(
            barrier, inc=1, device_id=place(partner(n - 1 - r)), device_id_type=pl.DeviceIdType.MESH
        ),
    )
    for load in loads:
        load.start()
    for load in loads:
        load.wait()

    def beam(b):
        total = None
        for p in range(num_slots):
            term = mm(w[b, p], rf[index_ref[0, b, p]], TN) * live_ref[0, b, p].astype(F32)
            total = term if total is None else total + term
        part[pl.ds(b * width, width), :] = total

    each(num_blocks, beam)
    pl.semaphore_wait(barrier, n - 1)

    sub, frame = lax.axis_index("sub"), lax.axis_index("frame")
    chan = lax.axis_index("chan")
    span = n_frame * vox

    def rows(c, s):
        return pl.ds(pl.multiple_of((c * n_sub + s) * span, span), span)

    def nth_chan(r):
        if n_chan <= 4:
            c, bit, flip = chan, 1, n_chan - 1 - r
            flip = flip ^ 1 if flip > 1 else flip
            while bit <= flip:
                if flip & bit:
                    c = c + bit - 2 * bit * lax.rem(chan // bit, 2)
                bit *= 2
            return c
        return lax.rem(chan + r + 1, n_chan)

    def exchange(r):
        c = nth_chan(r)
        return pltpu.make_async_remote_copy(
            src_ref=part.at[rows(c, 1 - sub), :],
            dst_ref=pair.at[r],
            send_sem=pair_send.at[r],
            recv_sem=pair_recv.at[r],
            device_id=(group, chan, frame, 1 - sub),
            device_id_type=pl.DeviceIdType.MESH,
        )

    each(n_chan, lambda r: exchange(r).start())
    mine = chan * n_frame + frame

    def scatter(r):
        c = nth_chan(r)
        exchange(r).wait_recv()
        sums[r] = pair[r] + part[rows(c, sub), :]
        for step in range(n_frame):
            q = lax.rem(frame + n_frame - 1 - step, n_frame)
            source = sums.at[r, pl.ds(pl.multiple_of(q * vox, vox), vox), :]

            def go():
                send(source, slots.at[mine], 0, (c * n_sub + sub) * n_frame + q).start()

            if n_chan <= 4 and r < n_chan - 1 or step < n_frame - 1:
                go()
            elif n_chan <= 4:
                slots[mine] = source[...]
            else:
                pl.when(r < n_chan - 1)(go)

    each(n_chan, scatter)
    if n_chan > 4:
        slots[mine] = sums[n_chan - 1, pl.ds(pl.multiple_of(frame * vox, vox), vox), :]
    peers = n_chan * n_frame
    got = slots.at[pl.ds(0, peers - 1)]
    send(got, got, 0, me).wait_recv()

    def gather_frame(q):
        if n <= 16:
            total = slots[q]
            for c in range(1, n_chan):
                total = total + slots[c * n_frame + q]
            return total
        return lax.fori_loop(1, n_chan, lambda c, t: t + slots[c * n_frame + q], slots[q])

    signal = jnp.concatenate([gather_frame(q) for q in range(n_frame)], axis=1)

    s_high, s_low = split(signal)
    t_high, t_low = split(start[...])
    rep_high = jnp.concatenate([s_high] * 4, axis=0)
    rep_low = jnp.concatenate([s_low] * 4, axis=0)
    proj = mm(t_high, rep_high, NT) + mm(t_low, rep_high, NT) + mm(t_high, rep_low, NT)
    p_high = proj.astype(BF16).astype(F32)
    lane = lax.broadcasted_iota(jnp.int32, proj.shape, 1)
    proj = jnp.where(lane < 2 * vox, p_high, proj - p_high).astype(BF16)
    sub_part = mm(proj, jnp.concatenate([s_high, s_low] * 2, axis=0), NN)
    for j in range(n_lane):
        mpart[j] = sub_part[:, j * LANES : (j + 1) * LANES]

    base = (n_chan // 2 - 1) * n_sub * n_frame
    units = n_lane * (RMAX // UNIT)
    reducer = (me >= base) & (me < base + units)

    def unit(ref, u):
        return ref.at[u // (RMAX // UNIT), pl.ds(pl.multiple_of(lax.rem(u, RMAX // UNIT) * UNIT, UNIT), UNIT), :]

    far = jnp.where(me < n // 2, units // 2, 0)

    def to_reducer(r):
        u = lax.rem(far + r, units)

        @pl.when(base + u != me)
        def _():
            send(unit(mpart, u), mslots.at[me], 1, base + u).start()

    each(units, to_reducer)

    @pl.when(reducer)
    def _():
        mine = me - base
        mslots[me] = unit(mpart, mine)[...]
        send(mslots.at[pl.ds(0, n - 1)], mslots.at[pl.ds(0, n - 1)], 1, me).wait_recv()
        if n <= 16:
            total = mslots[0]
            for d in range(1, n):
                total = total + mslots[d]
        else:
            total = lax.fori_loop(1, n, lambda d, t: t + mslots[d], mslots[0])
        unit(full, mine)[...] = total
        each(n - 1, lambda r: send(unit(full, mine), unit(full, mine), 2, partner(r + 1)).start())
        got = mslots.at[pl.ds(0, units - 1)]
        send(got, got, 2, me).wait_recv()

    @pl.when(jnp.logical_not(reducer))
    def _():
        got = mslots.at[pl.ds(0, units)]
        send(got, got, 2, me).wait_recv()

    kept = lax.broadcasted_iota(jnp.int32, (RMAX, 1), 0) < rank_ref[0, 0]
    space = jnp.concatenate([full[j] for j in range(n_lane)], axis=1)
    norm = jnp.sum(space * space, axis=1, keepdims=True)
    space = jnp.where(kept, space * lax.rsqrt(norm), 0.0)
    m_high, m_low = split(space)
    left_high = jnp.concatenate([m_high, s_high], axis=0)
    left_low = jnp.concatenate([m_low, s_low], axis=0)
    rep_high = jnp.concatenate([m_high] * 4, axis=0)
    rep_low = jnp.concatenate([m_low] * 4, axis=0)
    system = mm(left_high, rep_high, NT) + mm(left_low, rep_high, NT) + mm(left_high, rep_low, NT)
    row = lax.broadcasted_iota(jnp.int32, system.shape, 0)
    order = lax.rem(lax.broadcasted_iota(jnp.int32, system.shape, 1), RMAX)
    system = system + jnp.where((row == order) & (row >= rank_ref[0, 0]), 1.0, 0.0)
    order = order[:1]
    for panel in range(0, RMAX, SUBL):
        if panel:
            system = system[SUBL:, :]
        columns = [jnp.broadcast_to(system[:, panel + i : panel + i + 1], system.shape) for i in range(SUBL)]
        for i in range(0, SUBL, 2):
            column0, column1 = columns[i : i + 2]
            p00, p01, p11 = column0[i : i + 1, :], column1[i : i + 1, :], column1[i + 1 : i + 2, :]
            inverse = 1.0 / (p00 * p11 - p01 * p01)

            def update(target, row0, row1):
                factor0 = (p11 * row0 - p01 * row1) * inverse
                factor1 = (p00 * row1 - p01 * row0) * inverse
                return target - column0 * factor0 - column1 * factor1

            for j in range(i + 2, SUBL):
                columns[j] = update(columns[j], columns[j][i : i + 1, :], columns[j][i + 1 : i + 2, :])
            here0, here1 = order == panel + i, order == panel + i + 1
            row0 = jnp.where(here0, -1.0, jnp.where(here1, 0.0, system[i : i + 1, :]))
            row1 = jnp.where(here0, 0.0, jnp.where(here1, -1.0, system[i + 1 : i + 2, :]))
            system = update(jnp.where(here0 | here1, 0.0, system), row0, row1)
    coeffs = system[SUBL:, :]
    c_high = coeffs.astype(BF16).astype(F32)
    lane = lax.broadcasted_iota(jnp.int32, coeffs.shape, 1)
    coeffs = jnp.where(lane < 2 * RMAX, c_high, coeffs - c_high).astype(BF16)
    clean = signal - mm(coeffs, jnp.concatenate([m_high, m_low] * 2, axis=0), NN)
    power = jnp.sum(clean * clean, axis=1, keepdims=True) * (1.0 / clean.shape[1])
    diagonal = lax.broadcasted_iota(jnp.int32, (vox, vox), 0) == lax.broadcasted_iota(jnp.int32, (vox, vox), 1)
    out_ref[...] = jnp.sum(jnp.where(diagonal, power, 0.0), axis=0, keepdims=True)[None]

    sent = slots.at[pl.ds(0, peers - 1)]
    send(sent, sent, 0, me).wait_send()
    each(n_chan, lambda r: exchange(r).wait_send())

    @pl.when(reducer)
    def _():
        sent = mslots.at[pl.ds(0, units - 1)]
        send(sent, sent, 1, me).wait_send()
        sent = mslots.at[pl.ds(0, n - 1)]
        send(sent, sent, 2, me).wait_send()

    @pl.when(jnp.logical_not(reducer))
    def _():
        sent = mslots.at[pl.ds(0, units)]
        send(sent, sent, 1, me).wait_send()


def shards(dims, rf, weights, sample_block, live, rank):
    n = math.prod(dims)
    _, num_blocks, num_slots, depth, width = weights.shape
    vox = num_blocks * width // n
    frames = rf.shape[1] * dims[2]
    n_lane = frames // LANES
    rank = rank[None]
    blocks = rf.reshape(rf.shape[0] // depth, depth, rf.shape[1])
    hbm = pl.BlockSpec(memory_space=pl.ANY)
    return pl.pallas_call(
        functools.partial(kernel, dims),
        out_shape=pltpu.VMEM((1, 1, vox), F32),
        in_specs=[hbm] * 6,
        out_specs=pl.BlockSpec(memory_space=pltpu.VMEM),
        scratch_shapes=[
            pltpu.SMEM(sample_block.shape, jnp.int32),
            pltpu.SMEM(live.shape, jnp.int32),
            pltpu.SMEM(rank.shape, jnp.int32),
            pltpu.VMEM(blocks.shape, BF16),
            pltpu.VMEM(weights.shape[1:], BF16),
            pltpu.VMEM((RMAX, frames), F32),
            pltpu.VMEM((num_blocks * width, rf.shape[1]), F32),
            pltpu.VMEM((dims[0], dims[2] * vox, rf.shape[1]), F32),
            pltpu.VMEM((dims[0], dims[2] * vox, rf.shape[1]), F32),
            pltpu.VMEM((dims[0] * dims[2], vox, rf.shape[1]), F32),
            pltpu.VMEM((n_lane, RMAX, LANES), F32),
            pltpu.VMEM((n, UNIT, LANES), F32),
            pltpu.VMEM((n_lane, RMAX, LANES), F32),
            pltpu.SemaphoreType.DMA((6,)),
            pltpu.SemaphoreType.DMA((3,)),
            pltpu.SemaphoreType.DMA((3,)),
            pltpu.SemaphoreType.DMA((dims[0],)),
            pltpu.SemaphoreType.DMA((dims[0],)),
        ],
        compiler_params=pltpu.CompilerParams(
            collective_id=0, has_side_effects=True, vmem_limit_bytes=60 * 1024 * 1024
        ),
        name="power_doppler",
    )(sample_block, live, rank, blocks, weights[0], jnp.asarray(start_basis(frames)))


def solution(mesh):
    dims = (mesh.shape["chan"], mesh.shape["sub"], mesh.shape["frame"])
    return jax.shard_map(
        functools.partial(shards, dims),
        mesh=mesh,
        in_specs=(
            P(("group", "chan", "sub"), "frame"),
            P(("chan", "sub"), None, None, None, None),
            P(("chan", "sub"), None, None),
            P(("chan", "sub"), None, None),
            P("group"),
        ),
        out_specs=P(("group", "chan", "sub"), "frame", None),
        check_vma=False,
    )
```

```python
import functools
import math

import jax
import jax.numpy as jnp
import numpy as np
from jax import lax
from jax.experimental import pallas as pl
from jax.experimental.pallas import tpu as pltpu
from jax.sharding import PartitionSpec as P

RMAX = 32
LANES = 128
SUBL = 8
UNIT = 16
F32 = jnp.float32
BF16 = jnp.bfloat16
NT = (((1,), (1,)), ((), ()))
NN = (((1,), (0,)), ((), ()))
TN = (((0,), (0,)), ((), ()))


def start_basis(frames):
    at = np.arange(frames, dtype=np.float64)[None, :] + 0.5
    order = np.arange(RMAX, dtype=np.float64)[:, None]
    return (np.cos(math.pi * at * order / frames) * math.sqrt(2.0 / frames)).astype(np.float32)


def split(x):
    high = x.astype(BF16)
    return high, (x - high.astype(F32)).astype(BF16)


def mm(a, b, dims):
    return lax.dot_general(a, b, dims, preferred_element_type=F32)


def each(count, body):
    if count <= 16:
        for i in range(count):
            body(i)
    else:
        lax.fori_loop(0, count, lambda i, c: (body(i), c)[1], 0)


def kernel(
    dims,
    index_hbm,
    live_hbm,
    rank_hbm,
    rf_hbm,
    w_hbm,
    start_hbm,
    out_ref,
    index_ref,
    live_ref,
    rank_ref,
    rf,
    w,
    start,
    part,
    pair,
    sums,
    slots,
    mpart,
    mslots,
    full,
    load_sem,
    send_sem,
    recv_sem,
    pair_send,
    pair_recv,
):
    n_chan, n_sub, n_frame = dims
    n = n_chan * n_sub * n_frame
    num_blocks, num_slots, depth, width = w.shape
    vox = slots.shape[1]
    n_lane = full.shape[0]
    group = lax.axis_index("group")
    me = (lax.axis_index("chan") * n_sub + lax.axis_index("sub")) * n_frame + lax.axis_index("frame")

    def partner(r):
        if not isinstance(r, int):
            return lax.rem(me + r, n)
        d, bit = me, 1
        while bit <= r:
            if r & bit:
                d = d + bit - 2 * bit * lax.rem(me // bit, 2)
            bit *= 2
        return d

    def place(d):
        return (group, d // (n_sub * n_frame), lax.rem(d, n_frame), lax.rem(d // n_frame, n_sub))

    def send(src, dst, phase, d):
        return pltpu.make_async_remote_copy(
            src_ref=src,
            dst_ref=dst,
            send_sem=send_sem.at[phase],
            recv_sem=recv_sem.at[phase],
            device_id=place(d),
            device_id_type=pl.DeviceIdType.MESH,
        )

    loads = [
        pltpu.make_async_copy(src, dst, load_sem.at[i])
        for i, (src, dst) in enumerate(
            (
                (index_hbm, index_ref),
                (live_hbm, live_ref),
                (rank_hbm, rank_ref),
                (rf_hbm, rf),
                (w_hbm, w),
                (start_hbm, start),
            )
        )
    ]
    barrier = pltpu.get_barrier_semaphore()
    each(
        n - 1,
        lambda r: pl.semaphore_signal(
            barrier, inc=1, device_id=place(partner(n - 1 - r)), device_id_type=pl.DeviceIdType.MESH
        ),
    )
    for load in loads:
        load.start()
    for load in loads:
        load.wait()

    def beam(b):
        total = None
        for p in range(num_slots):
            term = mm(w[b, p], rf[index_ref[0, b, p]], TN) * live_ref[0, b, p].astype(F32)
            total = term if total is None else total + term
        part[pl.ds(b * width, width), :] = total

    each(num_blocks, beam)
    pl.semaphore_wait(barrier, n - 1)

    sub, frame = lax.axis_index("sub"), lax.axis_index("frame")
    chan = lax.axis_index("chan")
    span = n_frame * vox

    def rows(c, s):
        return pl.ds(pl.multiple_of((c * n_sub + s) * span, span), span)

    def nth_chan(r):
        if n_chan <= 4:
            c, bit, flip = chan, 1, n_chan - 1 - r
            flip = flip ^ 1 if flip > 1 else flip
            while bit <= flip:
                if flip & bit:
                    c = c + bit - 2 * bit * lax.rem(chan // bit, 2)
                bit *= 2
            return c
        return lax.rem(chan + r + 1, n_chan)

    def exchange(r):
        c = nth_chan(r)
        return pltpu.make_async_remote_copy(
            src_ref=part.at[rows(c, 1 - sub), :],
            dst_ref=pair.at[r],
            send_sem=pair_send.at[r],
            recv_sem=pair_recv.at[r],
            device_id=(group, chan, frame, 1 - sub),
            device_id_type=pl.DeviceIdType.MESH,
        )

    each(n_chan, lambda r: exchange(r).start())
    mine = chan * n_frame + frame

    def scatter(r):
        c = nth_chan(r)
        exchange(r).wait_recv()
        sums[r] = pair[r] + part[rows(c, sub), :]
        for step in range(n_frame):
            q = lax.rem(frame + n_frame - 1 - step, n_frame)
            source = sums.at[r, pl.ds(pl.multiple_of(q * vox, vox), vox), :]

            def go():
                send(source, slots.at[mine], 0, (c * n_sub + sub) * n_frame + q).start()

            if n_chan <= 4 and r < n_chan - 1 or step < n_frame - 1:
                go()
            elif n_chan <= 4:
                slots[mine] = source[...]
            else:
                pl.when(r < n_chan - 1)(go)

    each(n_chan, scatter)
    if n_chan > 4:
        slots[mine] = sums[n_chan - 1, pl.ds(pl.multiple_of(frame * vox, vox), vox), :]
    peers = n_chan * n_frame
    got = slots.at[pl.ds(0, peers - 1)]
    send(got, got, 0, me).wait_recv()

    def gather_frame(q):
        if n <= 16:
            total = slots[q]
            for c in range(1, n_chan):
                total = total + slots[c * n_frame + q]
            return total
        return lax.fori_loop(1, n_chan, lambda c, t: t + slots[c * n_frame + q], slots[q])

    signal = jnp.concatenate([gather_frame(q) for q in range(n_frame)], axis=1)

    s_high, s_low = split(signal)
    t_high, t_low = split(start[...])
    rep_high = jnp.concatenate([s_high] * 4, axis=0)
    rep_low = jnp.concatenate([s_low] * 4, axis=0)
    proj = mm(t_high, rep_high, NT) + mm(t_low, rep_high, NT) + mm(t_high, rep_low, NT)
    p_high = proj.astype(BF16).astype(F32)
    lane = lax.broadcasted_iota(jnp.int32, proj.shape, 1)
    proj = jnp.where(lane < 2 * vox, p_high, proj - p_high).astype(BF16)
    stacked = jnp.concatenate([s_high, s_low] * 2, axis=0)

    base = (n_chan // 2 - 1) * n_sub * n_frame
    units = n_lane * (RMAX // UNIT)
    reducer = (me >= base) & (me < base + units)

    def unit(ref, u):
        if isinstance(u, int):
            return ref.at[u // (RMAX // UNIT), pl.ds(u % (RMAX // UNIT) * UNIT, UNIT), :]
        return ref.at[u // (RMAX // UNIT), pl.ds(pl.multiple_of(lax.rem(u, RMAX // UNIT) * UNIT, UNIT), UNIT), :]

    def to_reducer(u):
        @pl.when(base + u != me)
        def _():
            send(unit(mpart, u), mslots.at[me], 1, base + u).start()

    per_lane = RMAX // UNIT
    for j in range(n_lane):
        mpart[j] = mm(proj, stacked[:, j * LANES : (j + 1) * LANES], NN)
        for u in range(j * per_lane, (j + 1) * per_lane):
            to_reducer(u)

    @pl.when(reducer)
    def _():
        mine = me - base
        mslots[me] = unit(mpart, mine)[...]
        send(mslots.at[pl.ds(0, n - 1)], mslots.at[pl.ds(0, n - 1)], 1, me).wait_recv()
        if n <= 16:
            total = mslots[0]
            for d in range(1, n):
                total = total + mslots[d]
        else:
            total = lax.fori_loop(1, n, lambda d, t: t + mslots[d], mslots[0])
        unit(full, mine)[...] = total
        each(n - 1, lambda r: send(unit(full, mine), unit(full, mine), 2, partner(r + 1)).start())
        got = mslots.at[pl.ds(0, units - 1)]
        send(got, got, 2, me).wait_recv()

    @pl.when(jnp.logical_not(reducer))
    def _():
        got = mslots.at[pl.ds(0, units)]
        send(got, got, 2, me).wait_recv()

    kept = lax.broadcasted_iota(jnp.int32, (RMAX, 1), 0) < rank_ref[0, 0]
    space = jnp.concatenate([full[j] for j in range(n_lane)], axis=1)
    norm = jnp.sum(space * space, axis=1, keepdims=True)
    space = jnp.where(kept, space * lax.rsqrt(norm), 0.0)
    m_high, m_low = split(space)
    left_high = jnp.concatenate([m_high, s_high], axis=0)
    left_low = jnp.concatenate([m_low, s_low], axis=0)
    rep_high = jnp.concatenate([m_high] * 4, axis=0)
    rep_low = jnp.concatenate([m_low] * 4, axis=0)
    system = mm(left_high, rep_high, NT) + mm(left_low, rep_high, NT) + mm(left_high, rep_low, NT)
    row = lax.broadcasted_iota(jnp.int32, system.shape, 0)
    order = lax.rem(lax.broadcasted_iota(jnp.int32, system.shape, 1), RMAX)
    system = system + jnp.where((row == order) & (row >= rank_ref[0, 0]), 1.0, 0.0)
    order = order[:1]
    for panel in range(0, RMAX, SUBL):
        if panel:
            system = system[SUBL:, :]
        columns = [jnp.broadcast_to(system[:, panel + i : panel + i + 1], system.shape) for i in range(SUBL)]
        for i in range(0, SUBL, 2):
            column0, column1 = columns[i : i + 2]
            p00, p01, p11 = column0[i : i + 1, :], column1[i : i + 1, :], column1[i + 1 : i + 2, :]
            inverse = 1.0 / (p00 * p11 - p01 * p01)

            def update(target, row0, row1):
                factor0 = (p11 * row0 - p01 * row1) * inverse
                factor1 = (p00 * row1 - p01 * row0) * inverse
                return target - column0 * factor0 - column1 * factor1

            for j in range(i + 2, SUBL):
                columns[j] = update(columns[j], columns[j][i : i + 1, :], columns[j][i + 1 : i + 2, :])
            here0, here1 = order == panel + i, order == panel + i + 1
            row0 = jnp.where(here0, -1.0, jnp.where(here1, 0.0, system[i : i + 1, :]))
            row1 = jnp.where(here0, 0.0, jnp.where(here1, -1.0, system[i + 1 : i + 2, :]))
            system = update(jnp.where(here0 | here1, 0.0, system), row0, row1)
    coeffs = system[SUBL:, :]
    c_high = coeffs.astype(BF16).astype(F32)
    lane = lax.broadcasted_iota(jnp.int32, coeffs.shape, 1)
    coeffs = jnp.where(lane < 2 * RMAX, c_high, coeffs - c_high).astype(BF16)
    clean = signal - mm(coeffs, jnp.concatenate([m_high, m_low] * 2, axis=0), NN)
    power = jnp.sum(clean * clean, axis=1, keepdims=True) * (1.0 / clean.shape[1])
    diagonal = lax.broadcasted_iota(jnp.int32, (vox, vox), 0) == lax.broadcasted_iota(jnp.int32, (vox, vox), 1)
    out_ref[...] = jnp.sum(jnp.where(diagonal, power, 0.0), axis=0, keepdims=True)[None]

    sent = slots.at[pl.ds(0, peers - 1)]
    send(sent, sent, 0, me).wait_send()
    each(n_chan, lambda r: exchange(r).wait_send())

    @pl.when(reducer)
    def _():
        sent = mslots.at[pl.ds(0, units - 1)]
        send(sent, sent, 1, me).wait_send()
        sent = mslots.at[pl.ds(0, n - 1)]
        send(sent, sent, 2, me).wait_send()

    @pl.when(jnp.logical_not(reducer))
    def _():
        sent = mslots.at[pl.ds(0, units)]
        send(sent, sent, 1, me).wait_send()


def shards(dims, rf, weights, sample_block, live, rank):
    n = math.prod(dims)
    _, num_blocks, num_slots, depth, width = weights.shape
    vox = num_blocks * width // n
    frames = rf.shape[1] * dims[2]
    n_lane = frames // LANES
    rank = rank[None]
    blocks = rf.reshape(rf.shape[0] // depth, depth, rf.shape[1])
    hbm = pl.BlockSpec(memory_space=pl.ANY)
    return pl.pallas_call(
        functools.partial(kernel, dims),
        out_shape=pltpu.VMEM((1, 1, vox), F32),
        in_specs=[hbm] * 6,
        out_specs=pl.BlockSpec(memory_space=pltpu.VMEM),
        scratch_shapes=[
            pltpu.SMEM(sample_block.shape, jnp.int32),
            pltpu.SMEM(live.shape, jnp.int32),
            pltpu.SMEM(rank.shape, jnp.int32),
            pltpu.VMEM(blocks.shape, BF16),
            pltpu.VMEM(weights.shape[1:], BF16),
            pltpu.VMEM((RMAX, frames), F32),
            pltpu.VMEM((num_blocks * width, rf.shape[1]), F32),
            pltpu.VMEM((dims[0], dims[2] * vox, rf.shape[1]), F32),
            pltpu.VMEM((dims[0], dims[2] * vox, rf.shape[1]), F32),
            pltpu.VMEM((dims[0] * dims[2], vox, rf.shape[1]), F32),
            pltpu.VMEM((n_lane, RMAX, LANES), F32),
            pltpu.VMEM((n, UNIT, LANES), F32),
            pltpu.VMEM((n_lane, RMAX, LANES), F32),
            pltpu.SemaphoreType.DMA((6,)),
            pltpu.SemaphoreType.DMA((3,)),
            pltpu.SemaphoreType.DMA((3,)),
            pltpu.SemaphoreType.DMA((dims[0],)),
            pltpu.SemaphoreType.DMA((dims[0],)),
        ],
        compiler_params=pltpu.CompilerParams(
            collective_id=0, has_side_effects=True, vmem_limit_bytes=60 * 1024 * 1024
        ),
        name="power_doppler",
    )(sample_block, live, rank, blocks, weights[0], jnp.asarray(start_basis(frames)))


def solution(mesh):
    dims = (mesh.shape["chan"], mesh.shape["sub"], mesh.shape["frame"])
    return jax.shard_map(
        functools.partial(shards, dims),
        mesh=mesh,
        in_specs=(
            P(("group", "chan", "sub"), "frame"),
            P(("chan", "sub"), None, None, None, None),
            P(("chan", "sub"), None, None),
            P(("chan", "sub"), None, None),
            P("group"),
        ),
        out_specs=P(("group", "chan", "sub"), "frame", None),
        check_vma=False,
    )
```
